32 devices in a mesh: groups: 2 (over y), ctx: 4 (over z), head: 4 (over x, core).
Axes of the slice: x: 2, y: 2, z: 4, core: 2. Of those that a mesh axis runs over, the one named last changes fastest.
Arguments:
- query_rows: bfloat16 [3072, 3072], P(('groups', 'ctx', 'head')), parts along dimension 0, may hold values from -150 to 150
- key_rows: bfloat16 [3072, 3072], P(('groups', 'ctx', 'head')), parts along dimension 0, may hold values from -6 to 6
- value_rows: bfloat16 [3072, 3072], P(('groups', 'ctx', 'head')), parts along dimension 0, may hold values from -6 to 6
- tile_mask: int32 [8, 27], P(('groups', 'ctx')), parts along dimension 0, may hold values from 0 to 1, as said below
Outputs:
- attended: bfloat16 [3072, 3072], P(('groups', 'ctx', 'head')), parts along dimension 0
The draws below stay inside these ranges and needn't reach their ends.
There are 2 independent parts, one for each index of `groups`. The reference program is written for one: setup_inputs(seed, part) draws one part's arguments, and reference() takes and returns one part's arrays. A program takes and returns all parts, laid end to end along the dimension named above; each array names one. Nothing has to cross between parts.
Inputs may be any that keep to these rules, and one draw needn't show every extreme that they name: `tile_mask`: entry o of row i is 1 only where the key tile of offset o lies inside the grid; entry 13 is always 1; a row has at most 4 ones, and some row has exactly 4.
All inputs are finite; a program needn't handle non-finite values.
Results may differ from the reference program's by a relative error of at most 0.0023.
Values may be sent and summed in bfloat16 or wider, within the bound.
A program may use at most 64 MiB of HBM per device.

```python
import math
import jax
import jax.numpy as jnp
from jax import lax

HEADS = 24
HDIM = 128
D = 3072
TILE = 384
NTT = 1
DH = 2
DW = 2
KEPT = 4
TOKENS = 1536


def paired_fields(key):
    folded = jax.random.fold_in(key, 7)
    draw_keys = jax.random.split(folded, 3)
    queries = jnp.clip(jax.random.normal(draw_keys[0], (TOKENS, HEADS * HDIM), jnp.float32), -6.0, 6.0)
    key_field = jnp.clip(jax.random.normal(draw_keys[1], (TOKENS, HEADS * HDIM), jnp.float32), -6.0, 6.0)
    spread = jnp.exp(jax.random.uniform(draw_keys[2], (TOKENS, HEADS, 1), jnp.float32, 0.0, math.log(8.0)))
    queries = (queries.reshape(TOKENS, HEADS, HDIM) * spread).reshape(TOKENS, HEADS * HDIM)
    return (queries, key_field)


def draw_query_rows(key, part):
    return paired_fields(key)[0].astype(jnp.bfloat16)


def draw_key_rows(key, part):
    return paired_fields(key)[1].astype(jnp.bfloat16)


def draw_tile_mask(key, part):
    folded = jax.random.fold_in(key, 11)
    draw_keys = jax.random.split(folded, 2)
    tile_count = DH * DW * NTT
    block_total = DH * DW
    rotation = DW // 2
    tile_index = jnp.arange(tile_count, dtype=jnp.int32)
    frame_pos = tile_index % NTT
    grid_pos = (tile_index // NTT - rotation) % block_total
    column = grid_pos % DW
    grid_row = grid_pos // DW
    offset = jnp.arange(27, dtype=jnp.int32)
    step_frame = offset // 9 - 1
    step_row = offset // 3 % 3 - 1
    step_col = offset % 3 - 1
    frame_to = frame_pos[:, None] + step_frame[None, :]
    row_to = grid_row[:, None] + step_row[None, :]
    col_to = column[:, None] + step_col[None, :]
    inside = (frame_to >= 0) & (frame_to < NTT) & (row_to >= 0) & (row_to < DH) & (col_to >= 0) & (col_to < DW)
    counts = jax.random.randint(draw_keys[0], (tile_count,), 1, KEPT + 1, jnp.int32)
    forced_pos = min(1, DH - 1) * DW + min(1, DW - 1)
    forced = (forced_pos + rotation) % block_total * NTT + min(1, NTT - 1)
    counts = jnp.where(tile_index == forced, KEPT, counts)
    priority_noise = jax.random.randint(draw_keys[1], (tile_count, 27), 0, 1 << 20, jnp.int32) * 32 + offset[None, :]
    priority = jnp.where(offset[None, :] == 13, -1, jnp.where(inside, priority_noise, (1 << 26) + offset[None, :]))
    ranking = jnp.argsort(jnp.argsort(priority, axis=1), axis=1)
    return ((ranking < counts[:, None]) & inside).astype(jnp.int32)


def level_of(stream_key, shape, shards, least, high):
    def one(dim, blocks):
        steps = jax.random.uniform(jax.random.fold_in(jax.random.fold_in(stream_key, 6), dim), (blocks,), jnp.float32, least / len(shards), high / len(shards))
        return jnp.repeat(jnp.exp(steps), shape[dim] // blocks).reshape((-1,) + (1,) * (len(shape) - dim - 1))

    level = one(*shards[0])
    for cut in shards[1:]:
        level = level * one(*cut)
    return level


def gaussian(own_key, shape, deviation, most, cuts=(), kind=jnp.bfloat16):
    factor_of = level_of(own_key, shape, cuts, -0.22, 0.18) if cuts else 1.0
    entries = jax.random.normal(own_key, shape, jnp.float32) * deviation * factor_of
    return jnp.minimum(jnp.maximum(entries, -most), most).astype(kind)


def setup_inputs(seed: int = 0, part: int = 0) -> dict:
    keys = jax.random.split(jax.random.key(seed), 5)
    part_keys = jax.random.split(jax.random.fold_in(keys[4], part), 5)
    query_rows = draw_query_rows(jax.random.fold_in(jax.random.fold_in(keys[4], part), 71), part)
    key_rows = draw_key_rows(jax.random.fold_in(jax.random.fold_in(keys[4], part), 71), part)
    value_rows = gaussian(part_keys[2], (TOKENS, D), 1.0, 6.0, ((0, 16),))
    tile_mask = draw_tile_mask(jax.random.fold_in(jax.random.fold_in(keys[4], part), 71), part)
    return {"query_rows": query_rows, "key_rows": key_rows, "value_rows": value_rows, "tile_mask": tile_mask}


def reference(query_rows, key_rows, value_rows, tile_mask):
    block_total = DH * DW
    rotation = DW // 2
    flat_shape = (block_total, NTT, TILE, HEADS, HDIM)
    grid_shape = (DH, DW, NTT, TILE, HEADS, HDIM)
    query_grid = jnp.roll(query_rows.reshape(flat_shape), -rotation, axis=0).reshape(grid_shape)
    key_grid = jnp.roll(key_rows.reshape(flat_shape), -rotation, axis=0).reshape(grid_shape)
    value_grid = jnp.roll(value_rows.reshape(flat_shape), -rotation, axis=0).reshape(grid_shape)
    padding = ((1, 1), (1, 1), (1, 1), (0, 0), (0, 0), (0, 0))
    key_padded = jnp.pad(key_grid, padding)
    value_padded = jnp.pad(value_grid, padding)
    mask_grid = jnp.roll(tile_mask.reshape(block_total, NTT, 27), -rotation, axis=0).reshape(DH, DW, NTT, 27)
    score_scale = 1.0 / math.sqrt(HDIM)
    zero_index = jnp.zeros((), jnp.int32)
    frame_steps = [0, 1, 2] if NTT > 1 else [1]
    first_col = 9 * frame_steps[0]
    col_count = 9 * len(frame_steps)

    def one_block(block_index):
        block_row = (block_index // DW).astype(jnp.int32)
        block_col = (block_index % DW).astype(jnp.int32)
        start = (block_row, block_col, zero_index, zero_index, zero_index, zero_index)
        extent = (3, 3, NTT + 2, TILE, HEADS, HDIM)
        key_window = lax.dynamic_slice(key_padded, start, extent)
        value_window = lax.dynamic_slice(value_padded, start, extent)
        query_block = lax.dynamic_slice(query_grid, start, (1, 1, NTT, TILE, HEADS, HDIM)).reshape(NTT, TILE, HEADS, HDIM)
        mask_rows = lax.dynamic_slice(mask_grid, (block_row, block_col, zero_index, zero_index), (1, 1, NTT, 27)).reshape(NTT, 27)
        mask_rows = mask_rows[:, first_col:first_col + col_count]
        key_stack = jnp.stack([key_window[:, :, shift_frame:shift_frame + NTT] for shift_frame in frame_steps])
        key_stack = jnp.moveaxis(key_stack, 3, 0).reshape(NTT, col_count * TILE, HEADS, HDIM)
        value_stack = jnp.stack([value_window[:, :, shift_frame:shift_frame + NTT] for shift_frame in frame_steps])
        value_stack = jnp.moveaxis(value_stack, 3, 0).reshape(NTT, col_count * TILE, HEADS, HDIM)
        scores = jnp.einsum('fqhd,fkhd->fhqk', query_block.astype(jnp.float32), key_stack.astype(jnp.float32)) * score_scale
        kept_mask = jnp.repeat(mask_rows == 1, TILE, axis=1)[:, None, None, :]
        row_peak = lax.optimization_barrier(jnp.max(jnp.where(kept_mask, scores, -jnp.inf), axis=3, keepdims=True))
        weight = jnp.exp(jnp.where(kept_mask, scores - row_peak, -jnp.inf))
        row_total = lax.optimization_barrier(jnp.sum(weight, axis=3, keepdims=True))
        rounded = lax.optimization_barrier(weight.astype(jnp.bfloat16)).astype(jnp.float32)
        mixed_heads = jnp.einsum('fhqk,fkhd->fhqd', rounded, value_stack.astype(jnp.float32)) / row_total
        return jnp.transpose(mixed_heads, (0, 2, 1, 3)).astype(jnp.bfloat16)
    blocks = lax.map(one_block, jnp.arange(block_total, dtype=jnp.int32))
    blocks = jnp.roll(blocks.reshape(block_total, NTT, TILE, HEADS, HDIM), rotation, axis=0)
    return blocks.reshape(TOKENS, HEADS * HDIM)
```

```python
import functools
import math

import jax
import jax.numpy as jnp
from jax import lax
from jax.experimental import pallas as pl
from jax.experimental.pallas import tpu as pltpu
from jax.sharding import PartitionSpec as P

HDIM = 128


def passed_along(block, axis, distance):
    devices = range(lax.axis_size(axis))
    route = [((i - distance) % len(devices), i) for i in devices]
    return lax.ppermute(block, axis, route)


def on_device(query_rows, key_rows, value_rows, tile_mask):
    cycle_size = lax.axis_size("ctx")
    grid_rows = max(2, cycle_size // 8)
    grid_cols = cycle_size // grid_rows
    query_local, key_local, value_local = (
        lax.all_to_all(query_rows, "head", split_axis=1, concat_axis=0, tiled=True),
        lax.all_to_all(key_rows, "head", split_axis=1, concat_axis=0, tiled=True),
        lax.all_to_all(value_rows, "head", split_axis=1, concat_axis=0, tiled=True),
    )
    feature_width = query_local.shape[1]
    head_count = feature_width // HDIM
    frames = tile_mask.shape[0]
    tile_len = query_local.shape[0] // frames
    key_value = jnp.stack([key_local, value_local]).reshape(2, frames, tile_len, feature_width)
    row_parts = [passed_along(key_value, "ctx", shift_by) for shift_by in (1, -1)]
    row_strip = jnp.stack([row_parts[0], key_value, row_parts[1]])
    column_parts = [
        passed_along(row_strip, "ctx", shift_by) for shift_by in (grid_cols, -grid_cols)
    ]
    window = jnp.stack([column_parts[0], row_strip, column_parts[1]])
    key_tiles = window[:, :, 0].reshape(9 * frames, tile_len, feature_width)
    value_tiles = window[:, :, 1].reshape(9 * frames, tile_len, feature_width)
    kept_mask = tile_mask == 1
    first_offset = 9
    slot_count = 9
    slots = range(first_offset, first_offset + slot_count)
    slot_kept = kept_mask[:, first_offset : first_offset + slot_count]
    static_source = [
        [slot % 9 * frames + min(max(frame + slot // 9 - 1, 0), frames - 1) for slot in slots]
        for frame in range(frames)
    ]
    kept_cols = jnp.repeat(slot_kept, tile_len, axis=1)[:, None, :]
    score_scale = 1.0 / math.sqrt(HDIM)

    def picked(tiles):
        return jnp.stack(
            [jnp.concatenate([tiles[tile] for tile in row]) for row in static_source]
        )

    def one_head(head_index):
        column_start = head_index * HDIM
        key_head = lax.dynamic_slice_in_dim(key_tiles, column_start, HDIM, 2)
        value_head = lax.dynamic_slice_in_dim(value_tiles, column_start, HDIM, 2)
        query_head = lax.dynamic_slice_in_dim(query_local, column_start, HDIM, 1).reshape(
            frames, tile_len, HDIM
        )
        picked_keys = picked(key_head)
        picked_values = picked(value_head)
        scores = (
            jnp.einsum("fqd,fkd->fqk", query_head, picked_keys, preferred_element_type=jnp.float32)
            * score_scale
        )
        row_peak = jnp.max(jnp.where(kept_cols, scores, -jnp.inf), axis=2, keepdims=True)
        weight = jnp.exp(jnp.where(kept_cols, scores - row_peak, -jnp.inf))
        row_total = jnp.sum(weight, axis=2, keepdims=True)
        rounded = weight.astype(jnp.bfloat16)
        mixed = jnp.einsum(
            "fqk,fkd->fqd", rounded, picked_values, preferred_element_type=jnp.float32
        )
        return (mixed / row_total).astype(jnp.bfloat16)

    result = lax.map(one_head, jnp.arange(head_count, dtype=jnp.int32))
    result = jnp.transpose(result, (1, 2, 0, 3)).reshape(frames * tile_len, feature_width)
    return lax.all_to_all(result, "head", split_axis=0, concat_axis=1, tiled=True)


MESH = pl.DeviceIdType.MESH
MASKED = -1e30


def window_kernel(
    places, heads, q_ref, k_ref, v_ref, m_ref, out_ref, qbuf, kvbuf, obuf, mbuf, bias,
    in_send, in_recv, own_sem, pair_send, pair_recv, o_send, o_recv, o_own, m_send, m_recv,
):
    tiles, chips = places
    blocks = tiles * chips
    rows = q_ref.shape[0]
    tile_rows = chips * rows
    z = lax.axis_index("ctx")
    lane = lax.axis_index("head")
    x = lax.div(lane, 2)
    core = lax.rem(lane, 2)
    here = z * chips + x

    def peer(dz, dx):
        pz = lax.rem(z + dz, tiles)
        px = lax.rem(x + dx, chips)
        return pz * chips + px, {"ctx": pz, "head": px * 2 + core}

    sibling = {"ctx": z, "head": x * 2 + 1 - core}
    distances = [2, 1, 3, 0]
    offsets = [(dz, dx) for dz in distances for dx in range(chips) if (dz, dx) != (0, 0)]

    def columns(place, h):
        return pl.ds(pl.multiple_of((place * heads + h) * HDIM, HDIM), HDIM)

    def slot(kind, h, place):
        if kind == 2:
            return qbuf.at[h, pl.ds(pl.multiple_of(place * rows, 16), rows)]
        return kvbuf.at[h, core, kind, pl.ds(pl.multiple_of(place * rows, 16), rows)]

    sources = (k_ref, v_ref, q_ref)

    def own_copy(kind, h):
        return pltpu.make_async_copy(
            sources[kind].at[:, columns(here, h)], slot(kind, h, here), own_sem.at[h, kind]
        )

    def in_copy(kind, h, offset):
        place, device = peer(*offset)
        return pltpu.make_async_remote_copy(
            src_ref=sources[kind].at[:, columns(place, h)],
            dst_ref=slot(kind, h, here),
            send_sem=in_send.at[h, kind, place],
            recv_sem=in_recv.at[h, kind, here],
            device_id=device,
            device_id_type=MESH,
        )

    def in_arrival(kind, h, offset):
        place, device = peer(*offset)
        return pltpu.make_async_remote_copy(
            src_ref=sources[kind].at[:, columns(place, h)],
            dst_ref=slot(kind, h, place),
            send_sem=in_send.at[h, kind, place],
            recv_sem=in_recv.at[h, kind, place],
            device_id=device,
            device_id_type=MESH,
        )

    def mask_copy(dz, sender):
        pz = lax.rem(z + dz, tiles)
        return pltpu.make_async_remote_copy(
            src_ref=mbuf.at[z],
            dst_ref=mbuf.at[z if sender else pz],
            send_sem=m_send.at[pz],
            recv_sem=m_recv.at[z if sender else pz],
            device_id={"ctx": pz, "head": lane},
            device_id_type=MESH,
        )

    def pair_copy(h, side):
        return pltpu.make_async_remote_copy(
            src_ref=kvbuf.at[h, core],
            dst_ref=kvbuf.at[h, side],
            send_sem=pair_send.at[h],
            recv_sem=pair_recv.at[h],
            device_id=sibling,
            device_id_type=MESH,
        )

    def out_copy(h, pz, px):
        place = pz * chips + px
        return pltpu.make_async_remote_copy(
            src_ref=obuf.at[h, pl.ds(pl.multiple_of(place * rows, 16), rows)],
            dst_ref=out_ref.at[:, columns(here, h)],
            send_sem=o_send.at[h, place],
            recv_sem=o_recv.at[h, here],
            device_id={"ctx": pz, "head": px * 2 + core},
            device_id_type=MESH,
        )

    def out_arrival(h, offset):
        place, device = peer(*offset)
        return pltpu.make_async_remote_copy(
            src_ref=obuf.at[h, pl.ds(pl.multiple_of(place * rows, 16), rows)],
            dst_ref=out_ref.at[:, columns(place, h)],
            send_sem=o_send.at[h, place],
            recv_sem=o_recv.at[h, place],
            device_id=device,
            device_id_type=MESH,
        )

    def out_own(h):
        return pltpu.make_async_copy(
            obuf.at[h, pl.ds(pl.multiple_of(here * rows, 16), rows)],
            out_ref.at[:, columns(here, h)],
            o_own.at[h],
        )

    barrier = pltpu.get_barrier_semaphore()
    for offset in offsets:
        pl.semaphore_signal(barrier, inc=1, device_id=peer(*offset)[1], device_id_type=MESH)
    pl.semaphore_signal(barrier, inc=1, device_id=sibling, device_id_type=MESH)

    mbuf[z] = jnp.zeros(mbuf.shape[1:], mbuf.dtype)
    mbuf[z, 0:1, 0 : m_ref.shape[1]] = m_ref[...]
    pl.semaphore_wait(barrier, len(offsets) + 1)

    def start_head(h, carry):
        for kind in range(3):
            for offset in offsets:
                in_copy(kind, h, offset).start()
            own_copy(kind, h).start()
        return carry

    start_head(0, 0)
    for dz in distances[:-1]:
        mask_copy(dz, True).start()
    lax.fori_loop(1, heads, start_head, 0)

    for dz in distances[:-1]:
        mask_copy(dz, False).wait_recv()
    grid_cols = 2
    spot = lax.broadcasted_iota(jnp.int32, (1, blocks * rows), 1)
    for query in range(tiles):
        query_spot = (query - grid_cols // 2) % tiles
        kept = mbuf[query][0:1, :]
        row = jnp.zeros((1, blocks * rows), jnp.float32)
        for key in range(tiles):
            key_spot = (key - grid_cols // 2) % tiles
            step_row = key_spot // grid_cols - query_spot // grid_cols
            step_col = key_spot % grid_cols - query_spot % grid_cols
            entry = 9 + 3 * (step_row + 1) + step_col + 1
            inside = (spot >= key * tile_rows) & (spot < (key + 1) * tile_rows)
            dropped = jnp.where(kept[:, entry : entry + 1] == 1, 0.0, MASKED)
            row = jnp.where(inside, dropped, row)
        bias[query] = row

    factor = math.log2(math.e) / math.sqrt(HDIM)

    def attend(h, pz):
        start = pl.multiple_of(pz * tile_rows, 16)
        query = qbuf[h, pl.ds(start, tile_rows), :]
        extra = bias[pz]
        scores = [
            lax.dot_general(
                query, kvbuf[h, side, 0], (((1,), (1,)), ((), ())),
                preferred_element_type=jnp.float32,
            )
            + extra
            for side in range(2)
        ]
        peak = jnp.maximum(*[jnp.max(s, axis=1, keepdims=True) for s in scores])
        weights = [jnp.exp2((s - peak) * factor) for s in scores]
        total = sum(jnp.sum(w, axis=1, keepdims=True) for w in weights)
        mixed = sum(
            jnp.dot(
                weights[side].astype(jnp.bfloat16), kvbuf[h, side, 1],
                preferred_element_type=jnp.float32,
            )
            for side in range(2)
        )
        obuf[h, pl.ds(start, tile_rows), :] = (mixed / total).astype(jnp.bfloat16)

    def run_head(h, carry):
        for kind in range(2):
            for offset in offsets:
                in_arrival(kind, h, offset).wait_recv()
            own_copy(kind, h).wait()
        pair_copy(h, core).start()
        for offset in offsets:
            in_arrival(2, h, offset).wait_recv()
        own_copy(2, h).wait()
        pair_copy(h, 1 - core).wait_recv()

        def run_tile(i, carry):
            pz = lax.rem(z + 2 + i, tiles)
            attend(h, pz)
            for px in range(chips):
                mine = pz * chips + px == here

                @pl.when(jnp.logical_not(mine))
                def _():
                    out_copy(h, pz, px).start()

                @pl.when(mine)
                def _():
                    out_own(h).start()

            return carry

        return lax.fori_loop(0, tiles, run_tile, carry)

    lax.fori_loop(0, heads, run_head, 0)

    def finish_head(h, carry):
        for kind in range(3):
            for offset in offsets:
                in_copy(kind, h, offset).wait_send()
        pair_copy(h, core).wait_send()
        for offset in offsets:
            out_arrival(h, offset).wait_send()
            out_arrival(h, offset).wait_recv()
        out_own(h).wait()
        return carry

    for dz in distances[:-1]:
        mask_copy(dz, True).wait_send()
    lax.fori_loop(0, heads, finish_head, 0)


def one_kernel(query_rows, key_rows, value_rows, tile_mask):
    tiles = lax.axis_size("ctx")
    chips = lax.axis_size("head") // 2
    blocks = tiles * chips
    rows, width = query_rows.shape
    heads = width // HDIM // blocks
    flops = 8 * heads * blocks * rows * blocks * rows * HDIM
    return pl.pallas_call(
        functools.partial(window_kernel, (tiles, chips), heads),
        out_shape=jax.ShapeDtypeStruct((rows, width), jnp.bfloat16),
        in_specs=[pl.BlockSpec(memory_space=pl.ANY)] * 3
        + [pl.BlockSpec(memory_space=pltpu.VMEM)],
        out_specs=pl.BlockSpec(memory_space=pltpu.VMEM),
        scratch_shapes=[
            pltpu.VMEM((heads, blocks * rows, HDIM), jnp.bfloat16),
            pltpu.VMEM((heads, 2, 2, blocks * rows, HDIM), jnp.bfloat16),
            pltpu.VMEM((heads, blocks * rows, HDIM), jnp.bfloat16),
            pltpu.VMEM((tiles, 8, 128), jnp.int32),
            pltpu.VMEM((tiles, 1, blocks * rows), jnp.float32),
            pltpu.SemaphoreType.DMA((heads, 3, blocks)),
            pltpu.SemaphoreType.DMA((heads, 3, blocks)),
            pltpu.SemaphoreType.DMA((heads, 3)),
            pltpu.SemaphoreType.DMA((heads,)),
            pltpu.SemaphoreType.DMA((heads,)),
            pltpu.SemaphoreType.DMA((heads, blocks)),
            pltpu.SemaphoreType.DMA((heads, blocks)),
            pltpu.SemaphoreType.DMA((heads,)),
            pltpu.SemaphoreType.DMA((tiles,)),
            pltpu.SemaphoreType.DMA((tiles,)),
        ],
        compiler_params=pltpu.CompilerParams(
            collective_id=0, has_side_effects=True, vmem_limit_bytes=48 * 1024 * 1024
        ),
        cost_estimate=pl.CostEstimate(
            flops=flops, bytes_accessed=8 * rows * width, transcendentals=0
        ),
    )(query_rows, key_rows, value_rows, tile_mask)


def solution(mesh):
    placed = (
        P(("groups", "ctx", "head"), None),
        P(("groups", "ctx", "head"), None),
        P(("groups", "ctx", "head"), None),
        P(("groups", "ctx"), None),
    )
    small = mesh.shape["ctx"] == 4 and mesh.shape["head"] % 2 == 0
    body = one_kernel if small else on_device
    return jax.shard_map(
        body,
        mesh=mesh,
        in_specs=placed,
        out_specs=P(("groups", "ctx", "head"), None),
        check_vma=False,
    )
```

```python
import functools
import math

import jax
import jax.numpy as jnp
from jax import lax
from jax.experimental import pallas as pl
from jax.experimental.pallas import tpu as pltpu
from jax.sharding import PartitionSpec as P

HDIM = 128


def passed_along(block, axis, distance):
    devices = range(lax.axis_size(axis))
    route = [((i - distance) % len(devices), i) for i in devices]
    return lax.ppermute(block, axis, route)


def on_device(query_rows, key_rows, value_rows, tile_mask):
    cycle_size = lax.axis_size("ctx")
    grid_rows = max(2, cycle_size // 8)
    grid_cols = cycle_size // grid_rows
    query_local, key_local, value_local = (
        lax.all_to_all(query_rows, "head", split_axis=1, concat_axis=0, tiled=True),
        lax.all_to_all(key_rows, "head", split_axis=1, concat_axis=0, tiled=True),
        lax.all_to_all(value_rows, "head", split_axis=1, concat_axis=0, tiled=True),
    )
    feature_width = query_local.shape[1]
    head_count = feature_width // HDIM
    frames = tile_mask.shape[0]
    tile_len = query_local.shape[0] // frames
    key_value = jnp.stack([key_local, value_local]).reshape(2, frames, tile_len, feature_width)
    row_parts = [passed_along(key_value, "ctx", shift_by) for shift_by in (1, -1)]
    row_strip = jnp.stack([row_parts[0], key_value, row_parts[1]])
    column_parts = [
        passed_along(row_strip, "ctx", shift_by) for shift_by in (grid_cols, -grid_cols)
    ]
    window = jnp.stack([column_parts[0], row_strip, column_parts[1]])
    key_tiles = window[:, :, 0].reshape(9 * frames, tile_len, feature_width)
    value_tiles = window[:, :, 1].reshape(9 * frames, tile_len, feature_width)
    kept_mask = tile_mask == 1
    first_offset = 9
    slot_count = 9
    slots = range(first_offset, first_offset + slot_count)
    slot_kept = kept_mask[:, first_offset : first_offset + slot_count]
    static_source = [
        [slot % 9 * frames + min(max(frame + slot // 9 - 1, 0), frames - 1) for slot in slots]
        for frame in range(frames)
    ]
    kept_cols = jnp.repeat(slot_kept, tile_len, axis=1)[:, None, :]
    score_scale = 1.0 / math.sqrt(HDIM)

    def picked(tiles):
        return jnp.stack(
            [jnp.concatenate([tiles[tile] for tile in row]) for row in static_source]
        )

    def one_head(head_index):
        column_start = head_index * HDIM
        key_head = lax.dynamic_slice_in_dim(key_tiles, column_start, HDIM, 2)
        value_head = lax.dynamic_slice_in_dim(value_tiles, column_start, HDIM, 2)
        query_head = lax.dynamic_slice_in_dim(query_local, column_start, HDIM, 1).reshape(
            frames, tile_len, HDIM
        )
        picked_keys = picked(key_head)
        picked_values = picked(value_head)
        scores = (
            jnp.einsum("fqd,fkd->fqk", query_head, picked_keys, preferred_element_type=jnp.float32)
            * score_scale
        )
        row_peak = jnp.max(jnp.where(kept_cols, scores, -jnp.inf), axis=2, keepdims=True)
        weight = jnp.exp(jnp.where(kept_cols, scores - row_peak, -jnp.inf))
        row_total = jnp.sum(weight, axis=2, keepdims=True)
        rounded = weight.astype(jnp.bfloat16)
        mixed = jnp.einsum(
            "fqk,fkd->fqd", rounded, picked_values, preferred_element_type=jnp.float32
        )
        return (mixed / row_total).astype(jnp.bfloat16)

    result = lax.map(one_head, jnp.arange(head_count, dtype=jnp.int32))
    result = jnp.transpose(result, (1, 2, 0, 3)).reshape(frames * tile_len, feature_width)
    return lax.all_to_all(result, "head", split_axis=0, concat_axis=1, tiled=True)


MESH = pl.DeviceIdType.MESH
MASKED = -1e30
held_from = 2


def window_kernel(
    places, heads, q_ref, k_ref, v_ref, m_ref, out_ref, qbuf, kvbuf, obuf, mbuf, mrow, bias,
    in_send, in_recv, own_sem, pair_send, pair_recv, o_send, o_recv, o_own, m_send, m_recv,
):
    tiles, chips = places
    blocks = tiles * chips
    rows = q_ref.shape[0]
    tile_rows = chips * rows
    z = lax.axis_index("ctx")
    lane = lax.axis_index("head")
    x = lax.div(lane, 2)
    core = lax.rem(lane, 2)
    here = z * chips + x

    def peer(dz, dx):
        pz = lax.rem(z + dz, tiles)
        px = lax.rem(x + dx, chips)
        return pz * chips + px, {"ctx": pz, "head": px * 2 + core}

    sibling = {"ctx": z, "head": x * 2 + 1 - core}
    odd = lax.rem(z, 2)
    distances = [2, 3 - 2 * odd, 1 + 2 * odd]
    offsets = [(dz, dx) for dz in distances for dx in range(chips)]
    offsets += [(0, dx) for dx in range(1, chips)]

    def columns(place, h):
        return pl.ds(pl.multiple_of((place * heads + h) * HDIM, HDIM), HDIM)

    def slot(kind, h, place):
        if kind == 2:
            return qbuf.at[h, pl.ds(pl.multiple_of(place * rows, 16), rows)]
        return kvbuf.at[h, core, kind, pl.ds(pl.multiple_of(place * rows, 16), rows)]

    sources = (k_ref, v_ref, q_ref)

    def own_copy(kind, h):
        return pltpu.make_async_copy(
            sources[kind].at[:, columns(here, h)], slot(kind, h, here), own_sem.at[h, kind]
        )

    def in_copy(kind, h, offset):
        place, device = peer(*offset)
        return pltpu.make_async_remote_copy(
            src_ref=sources[kind].at[:, columns(place, h)],
            dst_ref=slot(kind, h, here),
            send_sem=in_send.at[h, kind, place],
            recv_sem=in_recv.at[h, kind, here],
            device_id=device,
            device_id_type=MESH,
        )

    def query_arrival(h, pz, px):
        return in_arrival(2, h, None, (pz * chips + px, {"ctx": pz, "head": px * 2 + core}))

    def in_arrival(kind, h, offset, sender=None):
        place, device = sender or peer(*offset)
        return pltpu.make_async_remote_copy(
            src_ref=sources[kind].at[:, columns(place, h)],
            dst_ref=slot(kind, h, place),
            send_sem=in_send.at[h, kind, place],
            recv_sem=in_recv.at[h, kind, place],
            device_id=device,
            device_id_type=MESH,
        )

    def mask_copy(dz, sender):
        pz = lax.rem(z + dz, tiles)
        return pltpu.make_async_remote_copy(
            src_ref=mbuf.at[z],
            dst_ref=mbuf.at[z if sender else pz],
            send_sem=m_send.at[pz],
            recv_sem=m_recv.at[z if sender else pz],
            device_id={"ctx": pz, "head": lane},
            device_id_type=MESH,
        )

    def pair_copy(h, side):
        return pltpu.make_async_remote_copy(
            src_ref=kvbuf.at[h, core],
            dst_ref=kvbuf.at[h, side],
            send_sem=pair_send.at[h],
            recv_sem=pair_recv.at[h],
            device_id=sibling,
            device_id_type=MESH,
        )

    def out_copy(h, pz, px):
        place = pz * chips + px
        return pltpu.make_async_remote_copy(
            src_ref=obuf.at[h, pl.ds(pl.multiple_of(place * rows, 16), rows)],
            dst_ref=out_ref.at[:, columns(here, h)],
            send_sem=o_send.at[h, place],
            recv_sem=o_recv.at[h, here],
            device_id={"ctx": pz, "head": px * 2 + core},
            device_id_type=MESH,
        )

    def out_arrival(h, offset):
        place, device = peer(*offset)
        return pltpu.make_async_remote_copy(
            src_ref=obuf.at[h, pl.ds(pl.multiple_of(place * rows, 16), rows)],
            dst_ref=out_ref.at[:, columns(place, h)],
            send_sem=o_send.at[h, place],
            recv_sem=o_recv.at[h, place],
            device_id=device,
            device_id_type=MESH,
        )

    def out_own(h):
        return pltpu.make_async_copy(
            obuf.at[h, pl.ds(pl.multiple_of(here * rows, 16), rows)],
            out_ref.at[:, columns(here, h)],
            o_own.at[h],
        )

    barrier = pltpu.get_barrier_semaphore()
    for offset in offsets:
        pl.semaphore_signal(barrier, inc=1, device_id=peer(*offset)[1], device_id_type=MESH)
    pl.semaphore_signal(barrier, inc=1, device_id=sibling, device_id_type=MESH)

    own_mask = pltpu.make_async_copy(m_ref, mrow, o_own.at[0])
    own_mask.start()
    own_mask.wait()
    mbuf[z] = jnp.zeros(mbuf.shape[1:], mbuf.dtype)
    mbuf[z, 0:1, 0 : mrow.shape[1]] = mrow[...]
    pl.semaphore_wait(barrier, len(offsets) + 1)

    def start_head(h, carry):
        for kind in range(3):
            for offset in offsets:
                in_copy(kind, h, offset).start()
            own_copy(kind, h).start()
        return carry

    start_head(0, 0)
    for dz in distances:
        mask_copy(dz, True).start()
    lax.fori_loop(1, heads, start_head, 0)

    for dz in distances:
        mask_copy(dz, False).wait_recv()
    grid_cols = 2
    spot = lax.broadcasted_iota(jnp.int32, (1, blocks * rows), 1)
    for query in range(tiles):
        query_spot = (query - grid_cols // 2) % tiles
        kept = mbuf[query][0:1, :]
        row = jnp.zeros((1, blocks * rows), jnp.float32)
        for key in range(tiles):
            key_spot = (key - grid_cols // 2) % tiles
            step_row = key_spot // grid_cols - query_spot // grid_cols
            step_col = key_spot % grid_cols - query_spot % grid_cols
            entry = 9 + 3 * (step_row + 1) + step_col + 1
            inside = (spot >= key * tile_rows) & (spot < (key + 1) * tile_rows)
            dropped = jnp.where(kept[:, entry : entry + 1] == 1, 0.0, MASKED)
            row = jnp.where(inside, dropped, row)
        bias[query] = row

    factor = math.log2(math.e) / math.sqrt(HDIM)

    def attend(h, pz):
        start = pl.multiple_of(pz * tile_rows, 16)
        query = qbuf[h, pl.ds(start, tile_rows), :]
        extra = bias[pz]
        scores = [
            lax.dot_general(
                query, kvbuf[h, side, 0], (((1,), (1,)), ((), ())),
                preferred_element_type=jnp.float32,
            )
            + extra
            for side in range(2)
        ]
        peak = jnp.maximum(*[jnp.max(s, axis=1, keepdims=True) for s in scores])
        weights = [jnp.exp2((s - peak) * factor) for s in scores]
        total = sum(jnp.sum(w, axis=1, keepdims=True) for w in weights)
        mixed = sum(
            jnp.dot(
                weights[side].astype(jnp.bfloat16), kvbuf[h, side, 1],
                preferred_element_type=jnp.float32,
            )
            for side in range(2)
        )
        obuf[h, pl.ds(start, tile_rows), :] = (mixed / total).astype(jnp.bfloat16)

    def tile_at(i):
        by_order = distances[2] * (i == 2) + distances[1] * (i == 1) + 2 * (i == 0)
        return lax.rem(z + by_order, tiles)

    def send_tile(h, pz):
        for px in range(chips):
            mine = pz * chips + px == here

            @pl.when(jnp.logical_not(mine))
            def _():
                out_copy(h, pz, px).start()

            @pl.when(mine)
            def _():
                out_own(h).start()

    def run_head(h, carry):
        for kind in range(2):
            for offset in offsets:
                in_arrival(kind, h, offset).wait_recv()
            own_copy(kind, h).wait()
        pair_copy(h, core).start()
        pair_copy(h, 1 - core).wait_recv()

        @pl.when(h == heads - 1)
        def _():
            for i in range(held_from, tiles):
                send_tile(heads - 2, tile_at(i))

        def run_tile(i, carry):
            pz = tile_at(i)
            for px in range(chips):
                mine = pz * chips + px == here

                @pl.when(jnp.logical_not(mine))
                def _():
                    query_arrival(h, pz, px).wait_recv()

                @pl.when(mine)
                def _():
                    own_copy(2, h).wait()

            attend(h, pz)

            @pl.when(jnp.logical_or(h != heads - 2, i < held_from))
            def _():
                send_tile(h, pz)

            return carry

        return lax.fori_loop(0, tiles, run_tile, carry)

    lax.fori_loop(0, heads, run_head, 0)

    def finish_head(h, carry):
        for kind in range(3):
            for offset in offsets:
                in_copy(kind, h, offset).wait_send()
        pair_copy(h, core).wait_send()
        for offset in offsets:
            out_arrival(h, offset).wait_send()
            out_arrival(h, offset).wait_recv()
        out_own(h).wait()
        return carry

    for dz in distances:
        mask_copy(dz, True).wait_send()
    lax.fori_loop(0, heads, finish_head, 0)


def one_kernel(query_rows, key_rows, value_rows, tile_mask):
    tiles = lax.axis_size("ctx")
    chips = lax.axis_size("head") // 2
    blocks = tiles * chips
    rows, width = query_rows.shape
    heads = width // HDIM // blocks
    flops = 8 * heads * blocks * rows * blocks * rows * HDIM
    return pl.pallas_call(
        functools.partial(window_kernel, (tiles, chips), heads),
        out_shape=jax.ShapeDtypeStruct((rows, width), jnp.bfloat16),
        in_specs=[pl.BlockSpec(memory_space=pltpu.HBM)] * 4,
        out_specs=pl.BlockSpec(memory_space=pltpu.VMEM),
        scratch_shapes=[
            pltpu.VMEM((heads, blocks * rows, HDIM), jnp.bfloat16),
            pltpu.VMEM((heads, 2, 2, blocks * rows, HDIM), jnp.bfloat16),
            pltpu.VMEM((heads, blocks * rows, HDIM), jnp.bfloat16),
            pltpu.VMEM((tiles, 8, 128), jnp.int32),
            pltpu.VMEM(tile_mask.shape, jnp.int32),
            pltpu.VMEM((tiles, 1, blocks * rows), jnp.float32),
            pltpu.SemaphoreType.DMA((heads, 3, blocks)),
            pltpu.SemaphoreType.DMA((heads, 3, blocks)),
            pltpu.SemaphoreType.DMA((heads, 3)),
            pltpu.SemaphoreType.DMA((heads,)),
            pltpu.SemaphoreType.DMA((heads,)),
            pltpu.SemaphoreType.DMA((heads, blocks)),
            pltpu.SemaphoreType.DMA((heads, blocks)),
            pltpu.SemaphoreType.DMA((heads,)),
            pltpu.SemaphoreType.DMA((tiles,)),
            pltpu.SemaphoreType.DMA((tiles,)),
        ],
        compiler_params=pltpu.CompilerParams(
            collective_id=0, has_side_effects=True, vmem_limit_bytes=54272 * 1024
        ),
        cost_estimate=pl.CostEstimate(
            flops=flops, bytes_accessed=8 * rows * width, transcendentals=0
        ),
    )(query_rows, key_rows, value_rows, tile_mask)


def solution(mesh):
    placed = (
        P(("groups", "ctx", "head"), None),
        P(("groups", "ctx", "head"), None),
        P(("groups", "ctx", "head"), None),
        P(("groups", "ctx"), None),
    )
    small = mesh.shape["ctx"] == 4 and mesh.shape["head"] % 2 == 0
    body = one_kernel if small else on_device
    return jax.shard_map(
        body,
        mesh=mesh,
        in_specs=placed,
        out_specs=P(("groups", "ctx", "head"), None),
        check_vma=False,
    )
```
